1024 devices in a mesh: dp: 16 (over y, core), expert: 4 (over x), mp: 16 (over z).
Axes of the slice: x: 4, y: 8, z: 16, core: 2. Of those that a mesh axis runs over, the one named last changes fastest.
Arguments:
- grad_out: bfloat16 [8192, 3072], P(('dp', 'expert'), 'mp'), may hold values from -6 to 6
- routing: int32 [8192, 2], P(('dp', 'expert')), may hold values from 0 to 3, all different within a row; in each aligned block of 128 rows (0 to 127, 128 to 255, ...) at most 96 rows name the same one
- gates: float32 [8192, 2], P(('dp', 'expert')), may hold values from 0.1 to 1
- hidden: bfloat16 [16, 4, 384, 8192], P('dp', 'expert', None, 'mp'), may hold values from -6 to 6
- error: bfloat16 [16, 4, 8192, 3072], P('dp', 'expert', 'mp'), may hold values from -24 to 24
- q_init: float32 [4, 4, 3072], P('expert'), may hold values from -0.109375 to 0.109375
Outputs:
- p_factor: float32 [4, 4, 8192], P('expert', None, 'mp')
- q_factor: float32 [4, 4, 3072], P('expert')
The draws below stay inside these ranges and needn't reach their ends.
Inputs may be any that keep to these rules, and one draw needn't show every extreme that they name: `routing`: the two experts of a row differ. In the rows of one device no expert is named more than 96 times, and in some device's rows an expert is named exactly 96 times.
All inputs are finite; a program needn't handle non-finite values.
Results may differ from the reference program's by a relative error of at most 0.0032.
Values may be sent and summed in bfloat16 or wider, within the bound.
A program may use at most 32 MiB of HBM per device.

```python
import math
import jax
import jax.numpy as jnp
import numpy as np
from jax import lax

D = 3072
FF = 8192
RANK = 4
TOK_DEV = 128
EXPERTS = 4
CAP = 96
TOKENS = 8192
N_DP = 16
N_EXPERT = 4


def levels(key, dims, pieces, least, high):
    loudness = 1.0
    for dim, blocks in pieces:
        heights = jax.random.uniform(jax.random.fold_in(jax.random.fold_in(key, 6), dim), (blocks,), jnp.float32, least / len(pieces), high / len(pieces))
        loudness = loudness * jnp.repeat(jnp.exp(heights), dims[dim] // blocks).reshape((-1,) + (1,) * (len(dims) - 1 - dim))
    return loudness


def assign_block(key, own, number, rows, number_of, top, limit, skew):
    sequence = jax.random.permutation(key, number_of)
    packed, usual = shares(number_of, rows * top, limit, skew, True), shares(number_of, rows * top, limit, skew, False)
    places = jnp.arange(number_of)

    def named(tallies, rotation):
        used = int((tallies > 0).sum())
        fixed = max(1, used // 4)
        moved = fixed + (places - fixed + rotation * (used - fixed)) % max(1, number_of - fixed)
        return jnp.zeros((number_of,), jnp.int32).at[sequence[jnp.where(places < fixed, places, moved)]].set(jnp.asarray(tallies, jnp.int32))

    tallies = jnp.where(number % 4 == 0, named(packed, number // 4), named(usual, number - number // 4 - 1))
    mixed = jax.random.permutation(jax.random.fold_in(own, 3), number_of)
    donor, sink = mixed[0:number_of // 2 * 2:2], mixed[1:number_of // 2 * 2:2]
    margin = jnp.minimum(tallies[donor] - 1, limit - tallies[sink]) // 2
    margin = jnp.where((donor == sequence[0]) | (sink == sequence[0]) | (tallies[sink] == 0), 0, jnp.maximum(margin, 0))
    moved = jax.random.randint(jax.random.fold_in(own, 4), (number_of // 2,), 0, 1 << 20) % (margin + 1)
    tallies = tallies.at[donor].add(-moved).at[sink].add(moved)
    labels = jnp.searchsorted(jnp.cumsum(tallies), jnp.arange(rows * top), side="right").astype(jnp.int32)
    listing = labels.reshape(top, rows).T
    listing = listing[jax.random.permutation(jax.random.fold_in(own, 1), rows)]
    rotation = jax.random.randint(jax.random.fold_in(own, 2), (rows, 1), 0, top)
    return jnp.take_along_axis(listing, (jnp.arange(top)[None, :] + rotation) % top, axis=1)


def shares(amount, total, reach, slope, full):
    weights = [(1 << 20) // math.isqrt(grade ** slope) + 1 for grade in range(1, amount + 1)]
    largest = reach if full else min(reach, max(-(-total // amount), total * weights[0] // sum(weights)))
    least = 1 if total - largest >= amount - 1 else 0
    given, rest = [largest] + [least] * (amount - 1), total - largest - least * (amount - 1)
    while rest > 0:
        movable = [i for i in range(1, amount) if given[i] < largest] or [i for i in range(1, amount) if given[i] < reach]
        pool, left = sum([weights[i] for i in movable]), rest
        for i in movable:
            addition = min(reach - given[i], max(1, left * weights[i] // pool), rest)
            given[i] = given[i] + addition
            rest = rest - addition
    return np.array(given)


def scatter_about(rng, shape, scale, reach, cuts=(), held_as=jnp.bfloat16):
    values = jax.random.normal(rng, shape, jnp.float32) * scale
    if len(cuts) > 0:
        values = levels(rng, shape, cuts, -0.22, 0.18) * values
    return jnp.clip(values, min=-reach, max=reach).astype(held_as)


def setup_inputs(seed: int = 0) -> dict:
    arg_keys = jax.random.split(jax.random.key(seed), 7)
    grad_out = scatter_about(arg_keys[0], (TOKENS, D), 1.0, 6.0, ((0, 64), (1, 16)))
    routing_keys = jax.random.split(jax.random.fold_in(arg_keys[1], 1), TOKENS // TOK_DEV)
    routing_turns = jax.random.permutation(jax.random.fold_in(arg_keys[1], 3), TOKENS // TOK_DEV)
    routing = jax.vmap(lambda own, number: assign_block(jax.random.fold_in(arg_keys[1], 2), own, number, TOK_DEV, EXPERTS, 2, CAP, 2))(routing_keys, routing_turns).reshape((TOKENS, 2))
    gates = jnp.clip(jnp.exp(math.log(1.0) - 2.3025851 * jax.random.uniform(arg_keys[2], (TOKENS, 2), jnp.float32) ** levels(arg_keys[2], (TOKENS, 2), ((0, 64),), -0.2, 0.2)), 0.1, 1.0)
    hidden = scatter_about(arg_keys[3], (N_DP, EXPERTS, N_EXPERT * CAP, FF), 1.0, 6.0, ((0, 16), (1, 4), (3, 16)))
    error = scatter_about(arg_keys[4], (N_DP, EXPERTS, FF, D), 4.0, 24.0, ((0, 16), (1, 4), (2, 16)))
    q_init = scatter_about(arg_keys[5], (EXPERTS, RANK, D), D ** -0.5, 0.109375, ((0, 4),), jnp.float32)
    return {"grad_out": grad_out, "routing": routing, "gates": gates, "hidden": hidden, "error": error, "q_init": q_init}


precise = lax.Precision.HIGHEST

def dispatch_block(token_rows, routes_block, gates_block, groups, capacity):
    flat_ids = routes_block.reshape(-1).astype(jnp.int32)
    onehot = (flat_ids[:, None] == jnp.arange(groups, dtype=jnp.int32)[None, :]).astype(jnp.int32)
    before = (jnp.cumsum(onehot, axis=0) - onehot).astype(jnp.int32)
    slot_index = lax.optimization_barrier(jnp.sum(before * onehot, axis=1)).astype(jnp.int32)
    target = (flat_ids * capacity + slot_index).astype(jnp.int32)
    placement = (target[:, None] == jnp.arange(groups * capacity, dtype=jnp.int32)[None, :]).astype(jnp.bfloat16)
    weights = gates_block.reshape(-1)[:, None]
    doubled = jnp.repeat(token_rows, routes_block.shape[1], axis=0).astype(jnp.float32)
    scaled = (weights * doubled).astype(jnp.bfloat16)
    outgoing = jnp.einsum('rs,rd->sd', placement.astype(jnp.float32), scaled.astype(jnp.float32), preferred_element_type=jnp.float32)
    return outgoing.astype(jnp.bfloat16).reshape(groups, capacity, token_rows.shape[1])

def compress(incoming, hidden_all, error_all, q_start):

    def p_term(operands):
        rows_in, hidden_rows, error_rows = operands
        products = jnp.einsum('kd,rd->kr', q_start, rows_in.astype(jnp.float32), precision=precise)
        left = jnp.einsum('kr,rf->kf', products, hidden_rows.astype(jnp.float32), precision=precise)
        return left + jnp.einsum('kd,fd->kf', q_start, error_rows.astype(jnp.float32), precision=precise)
    p_raw = lax.optimization_barrier(jnp.sum(lax.map(p_term, (incoming, hidden_all, error_all)), axis=0))
    gram_matrix = jnp.dot(p_raw, p_raw.T, precision=precise)
    lower_factor = jnp.linalg.cholesky(gram_matrix)
    p_orth = lax.linalg.triangular_solve(lower_factor, p_raw, left_side=True, lower=True)

    def q_term(operands):
        rows_in, hidden_rows, error_rows = operands
        mixing = jnp.einsum('kf,rf->kr', p_orth, hidden_rows.astype(jnp.float32), precision=precise)
        right = jnp.einsum('kr,rd->kd', mixing, rows_in.astype(jnp.float32), precision=precise)
        return right + jnp.einsum('kf,fd->kd', p_orth, error_rows.astype(jnp.float32), precision=precise)
    q_total = lax.optimization_barrier(jnp.sum(lax.map(q_term, (incoming, hidden_all, error_all)), axis=0))
    return (p_orth * math.sqrt(FF), q_total / N_DP)

def reference(grad_out, routing, gates, hidden, error, q_init):
    block_count = N_DP * N_EXPERT

    def dispatch_one(token_rows, routes_block, gates_block):
        return dispatch_block(token_rows, routes_block, gates_block, EXPERTS, CAP)
    outgoing = jax.vmap(dispatch_one)(grad_out.reshape(block_count, TOK_DEV, D), routing.reshape(block_count, TOK_DEV, 2), gates.reshape(block_count, TOK_DEV, 2))
    outgoing = outgoing.reshape(N_DP, N_EXPERT, EXPERTS, CAP, D)
    incoming = jnp.transpose(outgoing, (2, 0, 1, 3, 4)).reshape(EXPERTS, N_DP, N_EXPERT * CAP, D)
    p_list = []
    q_list = []
    for expert_id in range(EXPERTS):
        p_one, q_one = compress(incoming[expert_id], hidden[:, expert_id], error[:, expert_id], q_init[expert_id])
        p_list.append(p_one)
        q_list.append(q_one)
    return (jnp.stack(p_list), jnp.stack(q_list))
```

```python
import functools
import math

import jax
import jax.numpy as jnp
from jax import lax
from jax.experimental import pallas as pl
from jax.experimental.pallas import tpu as pltpu
from jax.sharding import PartitionSpec as P

MESH = pl.DeviceIdType.MESH
F32 = jnp.float32
BF16 = jnp.bfloat16
NT = (((1,), (1,)), ((), ()))
NN = (((1,), (0,)), ((), ()))


def split(x):
    high = x.astype(BF16)
    low = (x - high.astype(F32)).astype(BF16)
    return jnp.concatenate([high, low], axis=0)


def mul(x, y, dims):
    both = lax.dot_general(split(x), y, dims, preferred_element_type=F32)
    return both[0:4] + both[4:8]


def total(ref):
    acc = ref[0]
    for i in range(1, ref.shape[0]):
        acc = acc + ref[i]
    return acc


def bytes_of(ref, sem):
    return pltpu.make_async_copy(ref, ref, sem)


def kernel(
    sizes, ff, cap,
    gT_hbm, rT_hbm, gateT_hbm, h_hbm, e_hbm, q_hbm,
    p_out, q_out,
    gT, rT, gateT, h, e, q,
    outT, incT, ipk, qe, zb, pb, xb, gb, pes, peb, vb, fb,
    load_sem, a_send, a_recv, b_send, b_recv, c_send, c_recv, d_send, d_recv, g_send, g_recv, w_send, w_recv,
    v_send, v_recv, f_send, f_recv, far_sem,
):
    n_dp, n_ex, n_mp = sizes
    d, s, m = lax.axis_index("dp"), lax.axis_index("expert"), lax.axis_index("mp")
    slots = h.shape[0]
    far = n_mp // 4

    def peer(axis, me, n, i):
        return {axis: lax.rem(me + i, n)}

    small = [(gT_hbm, gT), (rT_hbm, rT), (gateT_hbm, gateT), (q_hbm.at[0], q), (h_hbm.at[0, 0], h)]
    loads = [pltpu.make_async_copy(a, b, load_sem.at[i]) for i, (a, b) in enumerate(small)]
    rows = e.shape[0] // 4
    for i in range(4):
        part = pl.ds(i * rows, rows)
        loads.append(pltpu.make_async_copy(e_hbm.at[0, 0, part], e.at[part], load_sem.at[len(small) + i]))

    barrier = pltpu.get_barrier_semaphore()
    near = [i for i in range(1, n_mp) if min(i, n_mp - i) <= far]
    for i in near:
        pl.semaphore_signal(barrier, inc=1, device_id=peer("mp", m, n_mp, i), device_id_type=MESH)
    for i in range(1, n_dp):
        pl.semaphore_signal(barrier, inc=1, device_id=peer("dp", d, n_dp, i), device_id_type=MESH)
    for i in range(1, n_ex):
        pl.semaphore_signal(barrier, inc=1, device_id=peer("expert", s, n_ex, i), device_id_type=MESH)
    for copy in loads:
        copy.start()

    for i in range(3):
        loads[i].wait()
    tokens = gT.shape[1]
    feats = gT.shape[0]
    r0, r1 = rT[0:1, :], rT[1:2, :]
    g0, g1 = gateT[0:1, :], gateT[1:2, :]
    ids = lax.broadcasted_iota(jnp.int32, (8, tokens), 0)
    hits = jnp.where((ids == r0) | (ids == r1), 1.0, 0.0).astype(F32)
    row = lax.broadcasted_iota(jnp.int32, (tokens, tokens), 0)
    col = lax.broadcasted_iota(jnp.int32, (tokens, tokens), 1)
    earlier = jnp.where(row < col, 1.0, 0.0).astype(BF16)
    before = lax.dot_general(hits.astype(BF16), earlier, NN, preferred_element_type=F32)
    place = jnp.where(hits > 0.5, before, -1.0).astype(jnp.int32)
    grads = gT[...].astype(F32)
    for i in range(n_ex):
        gate = jnp.where(r0 == i, g0, 0.0) + jnp.where(r1 == i, g1, 0.0)
        scaled = (grads * gate).astype(BF16)
        placement = jnp.where(row == place[i : i + 1, :], 1.0, 0.0).astype(BF16)
        outT[i] = lax.dot_general(scaled, placement, NT, preferred_element_type=F32).astype(BF16)
    odd = lax.rem(m, 2)
    window = pl.ds(pl.multiple_of(64 * odd, 64), feats)
    edge = pl.ds(pl.multiple_of(feats * (1 - odd), 64), 64)
    for i in range(n_ex):
        incT[i, edge, :] = jnp.zeros((64, tokens), BF16)
    incT[s, window, :] = outT[s]
    gb[m] = jnp.zeros(gb.shape[1:], F32)

    pl.semaphore_wait(barrier, len(near) + n_dp - 1 + n_ex - 1)
    sends = []
    for i in range(1, n_ex):
        there = lax.rem(s + i, n_ex)
        pltpu.make_async_remote_copy(
            src_ref=outT.at[there], dst_ref=incT.at[s, window], send_sem=a_send, recv_sem=a_recv,
            device_id={"expert": there}, device_id_type=MESH,
        ).start()
    for i in (far, n_mp - far):
        pl.semaphore_signal(far_sem, inc=1, device_id=peer("mp", m, n_mp, i), device_id_type=MESH)

    loads[3].wait()
    start = pl.multiple_of(feats * m - 64 * odd, 128)
    q_win = q[:, pl.ds(start, 256)]
    lane = lax.broadcasted_iota(jnp.int32, (4, 256), 1)
    q_win = jnp.where((lane >= 64 * odd) & (lane < 64 * odd + feats), q_win, 0.0)
    q_two = split(q_win)

    def exchange(axis, me, n, buf, send_sem, recv_sem, src=None):
        for i in range(1, n):
            there = lax.rem(me + i, n)
            pltpu.make_async_remote_copy(
                src_ref=buf.at[me] if src is None else src.at[there], dst_ref=buf.at[me],
                send_sem=send_sem, recv_sem=recv_sem, device_id={axis: there}, device_id_type=MESH,
            ).start()

    bytes_of(outT.at[pl.ds(0, n_ex - 1)], a_recv).wait()
    z_parts = []
    for i in range(n_ex):
        both = lax.dot_general(q_two, incT[i], NN, preferred_element_type=F32)
        z_parts.append((both[0:4] + both[4:8])[:, 0:cap])
    zb[m] = jnp.concatenate(z_parts, axis=1)
    pl.semaphore_wait(far_sem, 2)
    exchange("mp", m, n_mp, zb, b_send, b_recv)

    q_all = split(q[...])
    for i in range(4):
        loads[5 + i].wait()
        both = lax.dot_general(q_all, e[i * rows : (i + 1) * rows, :], NT, preferred_element_type=F32)
        qe[:, i * rows : (i + 1) * rows] = both[0:4] + both[4:8]
    ipk[...] = jnp.concatenate([incT[i].astype(F32)[:, 0:cap] for i in range(n_ex)], axis=1).astype(BF16)
    loads[4].wait()

    bytes_of(zb.at[pl.ds(0, n_mp - 1)], b_recv).wait()
    pb[d] = mul(total(zb), h[...], NN) + qe[...]
    exchange("dp", d, n_dp, pb, c_send, c_recv)
    bytes_of(pb.at[pl.ds(0, n_dp - 1)], c_recv).wait()
    p_raw = total(pb)

    xb[m] = mul(p_raw, h[...], NT)
    exchange("mp", m, n_mp, xb, d_send, d_recv)

    both = lax.dot_general(split(p_raw), e[...], NN, preferred_element_type=F32)
    pe = both[0:4] + both[4:8]
    for i in range(n_mp):
        skip = 64 * (i % 2)
        part = pe[:, feats * i - skip : feats * i - skip + 256] if feats * i - skip + 256 <= pe.shape[1] else None
        pes[i] = jnp.where((lane >= skip) & (lane < skip + feats), part, 0.0)
    peb[m] = pes[m]
    exchange("mp", m, n_mp, peb, w_send, w_recv, src=pes)
    gram = lax.dot_general(p_raw, p_raw, NT, precision=lax.Precision.HIGHEST, preferred_element_type=F32)
    gb[m, :, 0:4] = gram
    exchange("mp", m, n_mp, gb, g_send, g_recv)

    bytes_of(xb.at[pl.ds(0, n_mp - 1)], d_recv).wait()
    right = mul(total(xb), ipk[...], NT)
    bytes_of(peb.at[pl.ds(0, n_mp - 1)], w_recv).wait()
    vb[d] = right + total(peb)
    exchange("dp", d, n_dp, vb, v_send, v_recv)

    bytes_of(gb.at[pl.ds(0, n_mp - 1)], g_recv).wait()
    g = total(gb)
    low = [[None] * 4 for _ in range(4)]
    inv = [None] * 4
    for i in range(4):
        for j in range(i + 1):
            acc = g[i : i + 1, j : j + 1]
            for k in range(j):
                acc = acc - low[i][k] * low[j][k]
            if i == j:
                root = jnp.sqrt(acc)
                inv[i] = 1.0 / root
            else:
                low[i][j] = acc * inv[j]

    def solve(x, scale):
        done = []
        for i in range(4):
            acc = x[i : i + 1, :]
            for k in range(i):
                acc = acc - low[i][k] * done[k]
            done.append(acc * inv[i])
        return jnp.concatenate(done, axis=0) * scale

    p_out[0] = solve(p_raw, math.sqrt(ff))

    bytes_of(vb.at[pl.ds(0, n_dp - 1)], v_recv).wait()
    fb[m] = solve(total(vb), 1.0 / n_dp)
    exchange("mp", m, n_mp, fb, f_send, f_recv)
    bytes_of(fb.at[pl.ds(0, n_mp - 1)], f_recv).wait()
    for i in range(0, n_mp, 2):
        even, uneven = fb[i], fb[i + 1]
        q_out[0, :, feats * i : feats * i + 128] = even[:, 0:128]
        q_out[0, :, feats * i + 128 : feats * i + 256] = even[:, 128:256] + uneven[:, 0:128]
        q_out[0, :, feats * i + 256 : feats * i + 384] = uneven[:, 128:256]

    bytes_of(outT.at[pl.ds(0, n_ex - 1)], a_send).wait()
    for buf, sem, n in ((zb, b_send, n_mp), (pb, c_send, n_dp), (xb, d_send, n_mp), (gb, g_send, n_mp),
                        (peb, w_send, n_mp), (vb, v_send, n_dp), (fb, f_send, n_mp)):
        bytes_of(buf.at[pl.ds(0, n - 1)], sem).wait()


def shards(grad_out, routing, gates, hidden, error, q_init):
    sizes = (lax.axis_size("dp"), lax.axis_size("expert"), lax.axis_size("mp"))
    n_dp, n_ex, n_mp = sizes
    tokens, feats = grad_out.shape
    slots, units = hidden.shape[2:]
    width = error.shape[3]
    rank = q_init.shape[1]
    dma = pltpu.SemaphoreType.DMA
    return pl.pallas_call(
        functools.partial(kernel, sizes, units * n_mp, slots // n_ex),
        out_shape=(
            jax.ShapeDtypeStruct((1, rank, units), F32),
            jax.ShapeDtypeStruct((1, rank, width), F32),
        ),
        in_specs=[pl.BlockSpec(memory_space=pltpu.HBM)] * 6,
        out_specs=(pl.BlockSpec(memory_space=pltpu.VMEM), pl.BlockSpec(memory_space=pltpu.VMEM)),
        scratch_shapes=[
            pltpu.VMEM((feats, tokens), BF16),
            pltpu.VMEM((2, tokens), jnp.int32),
            pltpu.VMEM((2, tokens), F32),
            pltpu.VMEM((slots, units), BF16),
            pltpu.VMEM((units, width), BF16),
            pltpu.VMEM((rank, width), F32),
            pltpu.VMEM((n_ex, feats, tokens), BF16),
            pltpu.VMEM((n_ex, 256, tokens), BF16),
            pltpu.VMEM((256, slots), BF16),
            pltpu.VMEM((rank, units), F32),
            pltpu.VMEM((n_mp, rank, slots), F32),
            pltpu.VMEM((n_dp, rank, units), F32),
            pltpu.VMEM((n_mp, rank, slots), F32),
            pltpu.VMEM((n_mp, rank, 128), F32),
            pltpu.VMEM((n_mp, rank, 256), F32),
            pltpu.VMEM((n_mp, rank, 256), F32),
            pltpu.VMEM((n_dp, rank, 256), F32),
            pltpu.VMEM((n_mp, rank, 256), F32),
            dma((9,)),
        ] + [dma(())] * 16 + [pltpu.SemaphoreType.REGULAR],
        compiler_params=pltpu.CompilerParams(
            collective_id=0, has_side_effects=True, vmem_limit_bytes=60 * 1024 * 1024
        ),
        name="compress",
    )(grad_out.T, routing.T, gates.T, hidden, error, q_init)


def solution(mesh):
    in_specs = (
        P(("dp", "expert"), "mp"),
        P(("dp", "expert"), None),
        P(("dp", "expert"), None),
        P("dp", "expert", None, "mp"),
        P("dp", "expert", "mp", None),
        P("expert", None, None),
    )
    out_specs = (P("expert", None, "mp"), P("expert", None, None))
    return jax.shard_map(shards, mesh=mesh, in_specs=in_specs, out_specs=out_specs, check_vma=False)
```

```python
import functools
import math

import jax
import jax.numpy as jnp
from jax import lax
from jax.experimental import pallas as pl
from jax.experimental.pallas import tpu as pltpu
from jax.sharding import PartitionSpec as P

MESH = pl.DeviceIdType.MESH
F32 = jnp.float32
BF16 = jnp.bfloat16
NT = (((1,), (1,)), ((), ()))
NN = (((1,), (0,)), ((), ()))


def split(x):
    high = x.astype(BF16)
    low = (x - high.astype(F32)).astype(BF16)
    return jnp.concatenate([high, low], axis=0)


def mul(x, y, dims):
    both = lax.dot_general(split(x), y, dims, preferred_element_type=F32)
    return both[0:4] + both[4:8]


def total(ref):
    acc = ref[0]
    for i in range(1, ref.shape[0]):
        acc = acc + ref[i]
    return acc


def bytes_of(ref, sem):
    return pltpu.make_async_copy(ref, ref, sem)


def kernel(
    sizes, ff, cap,
    gT_hbm, rT_hbm, gateT_hbm, h_hbm, e_hbm, q_hbm,
    p_out, q_out,
    gT, rT, gateT, h, e, q,
    outT, incT, ipk, qe, zb, pb, xb, pes, yb, ab, vb, fb, lb,
    load_sem, a_send, a_recv, b_send, b_recv, c_send, c_recv, d_send, d_recv, g_send, g_recv, y_send, y_recv,
    v_send, v_recv, f_send, f_recv, l_send, l_recv, far_sem,
):
    n_dp, n_ex, n_mp = sizes
    d, s, m = lax.axis_index("dp"), lax.axis_index("expert"), lax.axis_index("mp")
    slots = h.shape[0]
    far = n_mp // 4
    around = sorted(range(1, n_mp), key=lambda i: -min(i, n_mp - i))
    along = sorted(range(1, n_dp), key=lambda i: -min(i // 2, n_dp // 2 - i // 2))
    offsets = {"mp": around, "dp": along}

    def peer(axis, me, n, i):
        return {axis: lax.rem(me + i, n)}

    small = [(gT_hbm, gT), (rT_hbm, rT), (gateT_hbm, gateT), (q_hbm.at[0], q), (h_hbm.at[0, 0], h)]
    loads = [pltpu.make_async_copy(a, b, load_sem.at[i]) for i, (a, b) in enumerate(small)]
    rows = e.shape[0] // 4
    for i in range(4):
        part = pl.ds(i * rows, rows)
        loads.append(pltpu.make_async_copy(e_hbm.at[0, 0, part], e.at[part], load_sem.at[len(small) + i]))

    barrier = pltpu.get_barrier_semaphore()
    near = [i for i in around if min(i, n_mp - i) <= far]
    for copy in loads[0:3]:
        copy.start()
    for i in range(1, n_ex):
        pl.semaphore_signal(barrier, inc=1, device_id=peer("expert", s, n_ex, i), device_id_type=MESH)
    for i in near:
        pl.semaphore_signal(barrier, inc=1, device_id=peer("mp", m, n_mp, i), device_id_type=MESH)
    for i in along:
        pl.semaphore_signal(barrier, inc=1, device_id=peer("dp", d, n_dp, i), device_id_type=MESH)
    for copy in loads[3:]:
        copy.start()

    for i in range(3):
        loads[i].wait()
    tokens = gT.shape[1]
    feats = gT.shape[0]
    r0, r1 = rT[0:1, :], rT[1:2, :]
    g0, g1 = gateT[0:1, :], gateT[1:2, :]
    ids = lax.broadcasted_iota(jnp.int32, (8, tokens), 0)
    hits = jnp.where((ids == r0) | (ids == r1), 1.0, 0.0).astype(F32)
    row = lax.broadcasted_iota(jnp.int32, (tokens, tokens), 0)
    col = lax.broadcasted_iota(jnp.int32, (tokens, tokens), 1)
    earlier = jnp.where(row < col, 1.0, 0.0).astype(BF16)
    before = lax.dot_general(hits.astype(BF16), earlier, NN, preferred_element_type=F32)
    place = jnp.where(hits > 0.5, before, -1.0).astype(jnp.int32)
    grads = gT[...].astype(F32)
    for i in range(n_ex):
        gate = jnp.where(r0 == i, g0, 0.0) + jnp.where(r1 == i, g1, 0.0)
        scaled = (grads * gate).astype(BF16)
        placement = jnp.where(row == place[i : i + 1, :], 1.0, 0.0).astype(BF16)
        outT[i] = lax.dot_general(scaled, placement, NT, preferred_element_type=F32).astype(BF16)
    odd = lax.rem(m, 2)
    window = pl.ds(pl.multiple_of(64 * odd, 64), feats)
    edge = pl.ds(pl.multiple_of(feats * (1 - odd), 64), 64)
    for i in range(n_ex):
        incT[i, edge, :] = jnp.zeros((64, tokens), BF16)
    incT[s, window, :] = outT[s]

    pl.semaphore_wait(barrier, len(near) + n_dp - 1 + n_ex - 1)
    for i in sorted(range(1, n_ex), key=lambda i: -min(i, n_ex - i)):
        there = lax.rem(s + i, n_ex)
        pltpu.make_async_remote_copy(
            src_ref=outT.at[there], dst_ref=incT.at[s, window], send_sem=a_send, recv_sem=a_recv,
            device_id={"expert": there}, device_id_type=MESH,
        ).start()
    for i in (far, n_mp - far):
        pl.semaphore_signal(far_sem, inc=1, device_id=peer("mp", m, n_mp, i), device_id_type=MESH)

    loads[3].wait()
    start = pl.multiple_of(feats * m - 64 * odd, 128)
    q_win = q[:, pl.ds(start, 256)]
    lane = lax.broadcasted_iota(jnp.int32, (4, 256), 1)
    q_win = jnp.where((lane >= 64 * odd) & (lane < 64 * odd + feats), q_win, 0.0)
    q_two = split(q_win)

    def exchange(axis, me, n, buf, send_sem, recv_sem, src=None):
        for i in offsets[axis]:
            there = lax.rem(me + i, n)
            pltpu.make_async_remote_copy(
                src_ref=buf.at[me] if src is None else src.at[there], dst_ref=buf.at[me],
                send_sem=send_sem, recv_sem=recv_sem, device_id={axis: there}, device_id_type=MESH,
            ).start()

    bytes_of(outT.at[pl.ds(0, n_ex - 1)], a_recv).wait()
    z_parts = []
    for i in range(n_ex):
        both = lax.dot_general(q_two, incT[i], NN, preferred_element_type=F32)
        z_parts.append((both[0:4] + both[4:8])[:, 0:cap])
    zb[m] = jnp.concatenate(z_parts, axis=1)
    pl.semaphore_wait(far_sem, 2)
    exchange("mp", m, n_mp, zb, b_send, b_recv)

    q_all = split(q[...])
    for i in range(4):
        loads[5 + i].wait()
        both = lax.dot_general(q_all, e[i * rows : (i + 1) * rows, :], NT, preferred_element_type=F32)
        qe[:, i * rows : (i + 1) * rows] = both[0:4] + both[4:8]
    ipk[...] = jnp.concatenate([incT[i].astype(F32)[:, 0:cap] for i in range(n_ex)], axis=1).astype(BF16)
    loads[4].wait()

    bytes_of(zb.at[pl.ds(0, n_mp - 1)], b_recv).wait()
    pb[d] = mul(total(zb), h[...], NN) + qe[...]
    exchange("dp", d, n_dp, pb, c_send, c_recv)
    bytes_of(pb.at[pl.ds(0, n_dp - 1)], c_recv).wait()
    p_raw = total(pb)

    xb[m] = mul(p_raw, h[...], NT)
    exchange("mp", m, n_mp, xb, d_send, d_recv)

    both = lax.dot_general(split(p_raw), e[...], NN, preferred_element_type=F32)
    pe = both[0:4] + both[4:8]
    for i in range(n_dp):
        skip = 64 * (i % 2)
        part = pe[:, feats * i - skip : feats * i - skip + 256]
        pes[i] = jnp.where((lane >= skip) & (lane < skip + feats), part, 0.0)
    yb[d] = pes[d]
    exchange("dp", d, n_dp, yb, y_send, y_recv, src=pes)

    tiled = jnp.concatenate([p_raw] * 4, axis=0)
    gram = lax.dot_general(p_raw, tiled, NT, precision=lax.Precision.HIGHEST, preferred_element_type=F32)
    own = lax.broadcasted_iota(jnp.int32, (4, 16), 0) == lax.broadcasted_iota(jnp.int32, (4, 16), 1) // 4
    gram = jnp.sum(jnp.where(own, gram, 0.0), axis=0, keepdims=True)
    odd_d = lax.rem(d, 2)
    gap = jnp.zeros((1, 176), F32)
    spare = jnp.concatenate([gap, jnp.zeros((1, 16), F32), gram, jnp.zeros((1, 48), F32)], axis=1)
    spare = jnp.where(odd_d == 1, jnp.concatenate([gram, gap, jnp.zeros((1, 64), F32)], axis=1), spare)
    top = lax.broadcasted_iota(jnp.int32, (4, 256), 0) == 0

    bytes_of(yb.at[pl.ds(0, n_dp - 1)], y_recv).wait()
    ab[m] = total(yb) + jnp.where(top, spare, 0.0)
    exchange("mp", m, n_mp, ab, g_send, g_recv)

    bytes_of(xb.at[pl.ds(0, n_mp - 1)], d_recv).wait()
    vb[d] = mul(total(xb), ipk[...], NT)
    exchange("dp", d, n_dp, vb, v_send, v_recv)
    bytes_of(vb.at[pl.ds(0, n_dp - 1)], v_recv).wait()
    fb[m] = total(vb)
    exchange("mp", m, n_mp, fb, f_send, f_recv)

    bytes_of(ab.at[pl.ds(0, n_mp - 1)], g_recv).wait()
    mixed = total(ab)
    lb[d] = jnp.where((lane >= 64 * odd_d) & (lane < 64 * odd_d + feats), mixed, 0.0)
    exchange("dp", d, n_dp, lb, l_send, l_recv)

    g = jnp.where(odd_d == 1, mixed[0:1, 0:16], mixed[0:1, 192:208])
    low = [[None] * 4 for _ in range(4)]
    inv = [None] * 4
    for i in range(4):
        for j in range(i + 1):
            acc = g[:, 4 * i + j : 4 * i + j + 1]
            for k in range(j):
                acc = acc - low[i][k] * low[j][k]
            if i == j:
                inv[i] = 1.0 / jnp.sqrt(acc)
            else:
                low[i][j] = acc * inv[j]

    def solve(x, scale):
        done = []
        for i in range(4):
            acc = x[i : i + 1, :]
            for k in range(i):
                acc = acc - low[i][k] * done[k]
            done.append(acc * inv[i])
        return jnp.concatenate(done, axis=0) * scale

    p_out[0] = solve(p_raw, math.sqrt(ff))

    bytes_of(lb.at[pl.ds(0, n_dp - 1)], l_recv).wait()
    bytes_of(fb.at[pl.ds(0, n_mp - 1)], f_recv).wait()
    for i in range(0, n_mp, 2):
        even, uneven = fb[i] + lb[i], fb[i + 1] + lb[i + 1]
        three = jnp.concatenate([even[:, 0:128], even[:, 128:256] + uneven[:, 0:128], uneven[:, 128:256]], axis=1)
        q_out[0, :, feats * i : feats * i + 384] = solve(three, 1.0 / n_dp)

    bytes_of(outT.at[pl.ds(0, n_ex - 1)], a_send).wait()
    for buf, sem, n in ((zb, b_send, n_mp), (pb, c_send, n_dp), (xb, d_send, n_mp), (yb, y_send, n_dp),
                        (ab, g_send, n_mp), (vb, v_send, n_dp), (fb, f_send, n_mp), (lb, l_send, n_dp)):
        bytes_of(buf.at[pl.ds(0, n - 1)], sem).wait()


def shards(grad_out, routing, gates, hidden, error, q_init):
    sizes = (lax.axis_size("dp"), lax.axis_size("expert"), lax.axis_size("mp"))
    n_dp, n_ex, n_mp = sizes
    tokens, feats = grad_out.shape
    slots, units = hidden.shape[2:]
    width = error.shape[3]
    rank = q_init.shape[1]
    dma = pltpu.SemaphoreType.DMA
    return pl.pallas_call(
        functools.partial(kernel, sizes, units * n_mp, slots // n_ex),
        out_shape=(
            pltpu.VMEM((1, rank, units), F32),
            pltpu.VMEM((1, rank, width), F32),
        ),
        in_specs=[pl.BlockSpec(memory_space=pltpu.HBM)] * 6,
        out_specs=(pl.BlockSpec(memory_space=pltpu.VMEM), pl.BlockSpec(memory_space=pltpu.VMEM)),
        scratch_shapes=[
            pltpu.VMEM((feats, tokens), BF16),
            pltpu.VMEM((2, tokens), jnp.int32),
            pltpu.VMEM((2, tokens), F32),
            pltpu.VMEM((slots, units), BF16),
            pltpu.VMEM((units, width), BF16),
            pltpu.VMEM((rank, width), F32),
            pltpu.VMEM((n_ex, feats, tokens), BF16),
            pltpu.VMEM((n_ex, 256, tokens), BF16),
            pltpu.VMEM((256, slots), BF16),
            pltpu.VMEM((rank, units), F32),
            pltpu.VMEM((n_mp, rank, slots), F32),
            pltpu.VMEM((n_dp, rank, units), F32),
            pltpu.VMEM((n_mp, rank, slots), F32),
            pltpu.VMEM((n_dp, rank, 256), F32),
            pltpu.VMEM((n_dp, rank, 256), F32),
            pltpu.VMEM((n_mp, rank, 256), F32),
            pltpu.VMEM((n_dp, rank, 256), F32),
            pltpu.VMEM((n_mp, rank, 256), F32),
            pltpu.VMEM((n_dp, rank, 256), F32),
            dma((9,)),
        ] + [dma(())] * 18 + [pltpu.SemaphoreType.REGULAR],
        compiler_params=pltpu.CompilerParams(
            collective_id=0, has_side_effects=True, vmem_limit_bytes=60 * 1024 * 1024
        ),
        name="compress",
    )(grad_out.T, routing.T, gates.T, hidden, error, q_init)


def solution(mesh):
    in_specs = (
        P(("dp", "expert"), "mp"),
        P(("dp", "expert"), None),
        P(("dp", "expert"), None),
        P("dp", "expert", None, "mp"),
        P("dp", "expert", "mp", None),
        P("expert", None, None),
    )
    out_specs = (P("expert", None, "mp"), P("expert", None, None))
    return jax.shard_map(shards, mesh=mesh, in_specs=in_specs, out_specs=out_specs, check_vma=False)
```

```python
import functools
import math

import jax
import jax.numpy as jnp
from jax import lax
from jax.experimental import pallas as pl
from jax.experimental.pallas import tpu as pltpu
from jax.sharding import PartitionSpec as P

MESH = pl.DeviceIdType.MESH
F32 = jnp.float32
BF16 = jnp.bfloat16
NT = (((1,), (1,)), ((), ()))
NN = (((1,), (0,)), ((), ()))


def split(x):
    high = x.astype(BF16)
    low = (x - high.astype(F32)).astype(BF16)
    return jnp.concatenate([high, low], axis=0)


def mul(x, y, dims):
    both = lax.dot_general(split(x), y, dims, preferred_element_type=F32)
    return both[0:4] + both[4:8]


def total(ref):
    acc = ref[0].astype(F32)
    for i in range(1, ref.shape[0]):
        acc = acc + ref[i].astype(F32)
    return acc


def pack(x):
    parts = [x[:, i : i + 128] for i in range(0, x.shape[1], 128)]
    fill = 16 - 4 * len(parts)
    return jnp.concatenate(parts + [jnp.zeros((fill, 128), F32)], axis=0).astype(BF16)


def unpack(x, n):
    return jnp.concatenate([x[4 * i : 4 * i + 4] for i in range(n // 128)], axis=1)


def bytes_of(ref, sem):
    return pltpu.make_async_copy(ref, ref, sem)


def kernel(
    sizes, ff, cap,
    gT_hbm, rT_hbm, gateT_hbm, h_hbm, e_hbm, q_hbm,
    p_out, q_out,
    gT, rT, gateT, h, hT, e, q,
    outT, incT, ipk, qe, zb, pb, xb, pes, yb, ab, vb, fb, lb,
    load_sem, a_send, a_recv, b_send, b_recv, c_send, c_recv, d_send, d_recv, g_send, g_recv, y_send, y_recv,
    v_send, v_recv, f_send, f_recv, l_send, l_recv, far_sem,
):
    n_dp, n_ex, n_mp = sizes
    d, s, m = lax.axis_index("dp"), lax.axis_index("expert"), lax.axis_index("mp")
    slots = h.shape[0]
    far = n_mp // 4
    around = sorted(range(1, n_mp), key=lambda i: -min(i, n_mp - i))
    along = sorted(range(1, n_dp), key=lambda i: -min(i // 2, n_dp // 2 - i // 2))
    offsets = {"mp": around, "dp": along}

    def peer(axis, me, n, i):
        return {axis: lax.rem(me + i, n)}

    small = [(gT_hbm, gT), (rT_hbm, rT), (gateT_hbm, gateT), (q_hbm.at[0], q), (h_hbm.at[0, 0], h)]
    loads = [pltpu.make_async_copy(a, b, load_sem.at[i]) for i, (a, b) in enumerate(small)]
    rows = e.shape[0] // 4
    for i in range(4):
        part = pl.ds(i * rows, rows)
        loads.append(pltpu.make_async_copy(e_hbm.at[0, 0, part], e.at[part], load_sem.at[len(small) + i]))

    barrier = pltpu.get_barrier_semaphore()
    near = [i for i in around if min(i, n_mp - i) <= far]
    for copy in loads[0:3]:
        copy.start()
    for i in range(1, n_ex):
        pl.semaphore_signal(barrier, inc=1, device_id=peer("expert", s, n_ex, i), device_id_type=MESH)
    for i in near:
        pl.semaphore_signal(barrier, inc=1, device_id=peer("mp", m, n_mp, i), device_id_type=MESH)
    for i in along:
        pl.semaphore_signal(barrier, inc=1, device_id=peer("dp", d, n_dp, i), device_id_type=MESH)
    for copy in loads[3:]:
        copy.start()

    for i in range(3):
        loads[i].wait()
    tokens = gT.shape[1]
    feats = gT.shape[0]
    r0, r1 = rT[0:1, :], rT[1:2, :]
    g0, g1 = gateT[0:1, :], gateT[1:2, :]
    ids = lax.broadcasted_iota(jnp.int32, (8, tokens), 0)
    hits = jnp.where((ids == r0) | (ids == r1), 1.0, 0.0).astype(F32)
    row = lax.broadcasted_iota(jnp.int32, (tokens, tokens), 0)
    col = lax.broadcasted_iota(jnp.int32, (tokens, tokens), 1)
    earlier = jnp.where(row < col, 1.0, 0.0).astype(BF16)
    before = lax.dot_general(hits.astype(BF16), earlier, NN, preferred_element_type=F32)
    place = jnp.where(hits > 0.5, before, -1.0).astype(jnp.int32)
    grads = gT[...].astype(F32)
    for i in range(n_ex):
        gate = jnp.where(r0 == i, g0, 0.0) + jnp.where(r1 == i, g1, 0.0)
        scaled = (grads * gate).astype(BF16)
        placement = jnp.where(row == place[i : i + 1, :], 1.0, 0.0).astype(BF16)
        outT[i] = lax.dot_general(scaled, placement, NT, preferred_element_type=F32).astype(BF16)
    odd = lax.rem(m, 2)
    window = pl.ds(pl.multiple_of(64 * odd, 64), feats)
    edge = pl.ds(pl.multiple_of(feats * (1 - odd), 64), 64)
    for i in range(n_ex):
        incT[i, edge, :] = jnp.zeros((64, tokens), BF16)
    incT[s, window, :] = outT[s]

    pl.semaphore_wait(barrier, len(near) + n_dp - 1 + n_ex - 1)
    for i in sorted(range(1, n_ex), key=lambda i: -min(i, n_ex - i)):
        there = lax.rem(s + i, n_ex)
        pltpu.make_async_remote_copy(
            src_ref=outT.at[there], dst_ref=incT.at[s, window], send_sem=a_send, recv_sem=a_recv,
            device_id={"expert": there}, device_id_type=MESH,
        ).start()
    for i in (far, n_mp - far):
        pl.semaphore_signal(far_sem, inc=1, device_id=peer("mp", m, n_mp, i), device_id_type=MESH)

    loads[3].wait()
    start = pl.multiple_of(feats * m - 64 * odd, 128)
    q_win = q[:, pl.ds(start, 256)]
    lane = lax.broadcasted_iota(jnp.int32, (4, 256), 1)
    q_win = jnp.where((lane >= 64 * odd) & (lane < 64 * odd + feats), q_win, 0.0)
    q_two = split(q_win)

    def exchange(axis, me, n, buf, send_sem, recv_sem, src=None):
        for i in offsets[axis]:
            there = lax.rem(me + i, n)
            pltpu.make_async_remote_copy(
                src_ref=buf.at[me] if src is None else src.at[there], dst_ref=buf.at[me],
                send_sem=send_sem, recv_sem=recv_sem, device_id={axis: there}, device_id_type=MESH,
            ).start()

    bytes_of(outT.at[pl.ds(0, n_ex - 1)], a_recv).wait()
    z_parts = []
    for i in range(n_ex):
        both = lax.dot_general(q_two, incT[i], NN, preferred_element_type=F32)
        z_parts.append((both[0:4] + both[4:8])[:, 0:cap])
    zb[m] = pack(jnp.concatenate(z_parts, axis=1))
    pl.semaphore_wait(far_sem, 2)
    exchange("mp", m, n_mp, zb, b_send, b_recv)

    q_all = split(q[...])
    for i in range(4):
        loads[5 + i].wait()
        both = lax.dot_general(q_all, e[i * rows : (i + 1) * rows, :], NT, preferred_element_type=F32)
        qe[:, i * rows : (i + 1) * rows] = both[0:4] + both[4:8]
    for i in range(n_ex):
        ipk[i * cap : (i + 1) * cap, :] = incT[i].T[0:cap, :]
    loads[4].wait()
    hT[...] = h[...].T

    bytes_of(zb.at[pl.ds(0, n_mp - 1)], b_recv).wait()
    pb[d] = mul(unpack(total(zb), slots), h[...], NN) + qe[...]
    exchange("dp", d, n_dp, pb, c_send, c_recv)
    bytes_of(pb.at[pl.ds(0, n_dp - 1)], c_recv).wait()
    p_raw = total(pb)

    xb[m] = pack(mul(p_raw, hT[...], NN))
    exchange("mp", m, n_mp, xb, d_send, d_recv)

    both = lax.dot_general(split(p_raw), e[...], NN, preferred_element_type=F32)
    pe = both[0:4] + both[4:8]
    quarters = n_dp // 4
    width = pe.shape[1] // quarters
    for i in range(n_dp):
        k, c = i // quarters, i % quarters
        pes[i] = pe[k : k + 1, c * width : (c + 1) * width]
    yb[d] = pes[d]
    exchange("dp", d, n_dp, yb, y_send, y_recv, src=pes)

    tiled = jnp.concatenate([p_raw] * 4, axis=0)
    gram = lax.dot_general(p_raw, tiled, NT, precision=lax.Precision.HIGHEST, preferred_element_type=F32)
    own = lax.broadcasted_iota(jnp.int32, (4, 16), 0) == lax.broadcasted_iota(jnp.int32, (4, 16), 1) // 4
    gram = jnp.sum(jnp.where(own, gram, 0.0), axis=0, keepdims=True)
    gram = jnp.concatenate([gram, jnp.zeros((1, 112), F32)], axis=1)

    bytes_of(yb.at[pl.ds(0, n_dp - 1)], y_recv).wait()
    ab[m] = jnp.concatenate([total(yb), gram], axis=1)
    exchange("mp", m, n_mp, ab, g_send, g_recv)

    bytes_of(xb.at[pl.ds(0, n_mp - 1)], d_recv).wait()
    vb[d] = mul(unpack(total(xb), slots), ipk[...], NN)
    exchange("dp", d, n_dp, vb, v_send, v_recv)
    bytes_of(vb.at[pl.ds(0, n_dp - 1)], v_recv).wait()
    fb[m] = total(vb)
    exchange("mp", m, n_mp, fb, f_send, f_recv)

    bytes_of(ab.at[pl.ds(0, n_mp - 1)], g_recv).wait()
    mixed = total(ab)
    lb[d] = mixed[:, 0:width]
    exchange("dp", d, n_dp, lb, l_send, l_recv)

    g = mixed[:, width : width + 16]
    low = [[None] * 4 for _ in range(4)]
    inv = [None] * 4
    for i in range(4):
        for j in range(i + 1):
            acc = g[:, 4 * i + j : 4 * i + j + 1]
            for k in range(j):
                acc = acc - low[i][k] * low[j][k]
            if i == j:
                inv[i] = 1.0 / jnp.sqrt(acc)
            else:
                low[i][j] = acc * inv[j]

    def solve(x, scale):
        done = []
        for i in range(4):
            acc = x[i]
            for k in range(i):
                acc = acc - low[i][k] * done[k]
            done.append(acc * inv[i])
        return jnp.concatenate(done, axis=0) * scale

    p_out[0] = solve([p_raw[i : i + 1, :] for i in range(4)], math.sqrt(ff))

    bytes_of(lb.at[pl.ds(0, n_dp - 1)], l_recv).wait()
    bytes_of(fb.at[pl.ds(0, n_mp - 1)], f_recv).wait()
    for i in range(0, n_mp, 2):
        even, uneven = fb[i], fb[i + 1]
        three = jnp.concatenate([even[:, 0:128], even[:, 128:256] + uneven[:, 0:128], uneven[:, 128:256]], axis=1)
        c, at = divmod(feats * i, width)
        x = [three[k : k + 1, :] + lb[k * quarters + c][:, at : at + 384] for k in range(4)]
        q_out[0, :, feats * i : feats * i + 384] = solve(x, 1.0 / n_dp)

    bytes_of(outT.at[pl.ds(0, n_ex - 1)], a_send).wait()
    for buf, sem, n in ((zb, b_send, n_mp), (pb, c_send, n_dp), (xb, d_send, n_mp), (yb, y_send, n_dp),
                        (ab, g_send, n_mp), (vb, v_send, n_dp), (fb, f_send, n_mp), (lb, l_send, n_dp)):
        bytes_of(buf.at[pl.ds(0, n - 1)], sem).wait()


def shards(grad_out, routing, gates, hidden, error, q_init):
    sizes = (lax.axis_size("dp"), lax.axis_size("expert"), lax.axis_size("mp"))
    n_dp, n_ex, n_mp = sizes
    tokens, feats = grad_out.shape
    slots, units = hidden.shape[2:]
    width = error.shape[3]
    rank = q_init.shape[1]
    piece = rank * width // n_dp
    dma = pltpu.SemaphoreType.DMA
    return pl.pallas_call(
        functools.partial(kernel, sizes, units * n_mp, slots // n_ex),
        out_shape=(
            pltpu.VMEM((1, rank, units), F32),
            pltpu.VMEM((1, rank, width), F32),
        ),
        in_specs=[pl.BlockSpec(memory_space=pltpu.HBM)] * 6,
        out_specs=(pl.BlockSpec(memory_space=pltpu.VMEM), pl.BlockSpec(memory_space=pltpu.VMEM)),
        scratch_shapes=[
            pltpu.VMEM((feats, tokens), BF16),
            pltpu.VMEM((2, tokens), jnp.int32),
            pltpu.VMEM((2, tokens), F32),
            pltpu.VMEM((slots, units), BF16),
            pltpu.VMEM((units, slots), BF16),
            pltpu.VMEM((units, width), BF16),
            pltpu.VMEM((rank, width), F32),
            pltpu.VMEM((n_ex, feats, tokens), BF16),
            pltpu.VMEM((n_ex, 256, tokens), BF16),
            pltpu.VMEM((slots, 256), BF16),
            pltpu.VMEM((rank, units), F32),
            pltpu.VMEM((n_mp, 16, 128), BF16),
            pltpu.VMEM((n_dp, rank, units), F32),
            pltpu.VMEM((n_mp, 16, 128), BF16),
            pltpu.VMEM((n_dp, 1, piece), F32),
            pltpu.VMEM((n_dp, 1, piece), F32),
            pltpu.VMEM((n_mp, 1, piece + 128), F32),
            pltpu.VMEM((n_dp, rank, 256), F32),
            pltpu.VMEM((n_mp, rank, 256), F32),
            pltpu.VMEM((n_dp, 1, piece), F32),
            dma((9,)),
        ] + [dma(())] * 18 + [pltpu.SemaphoreType.REGULAR],
        compiler_params=pltpu.CompilerParams(
            collective_id=0, has_side_effects=True, vmem_limit_bytes=60 * 1024 * 1024
        ),
        name="compress",
    )(grad_out.T, routing.T, gates.T, hidden, error, q_init)


def solution(mesh):
    in_specs = (
        P(("dp", "expert"), "mp"),
        P(("dp", "expert"), None),
        P(("dp", "expert"), None),
        P("dp", "expert", None, "mp"),
        P("dp", "expert", "mp", None),
        P("expert", None, None),
    )
    out_specs = (P("expert", None, "mp"), P("expert", None, None))
    return jax.shard_map(shards, mesh=mesh, in_specs=in_specs, out_specs=out_specs, check_vma=False)
```
